32 devices in a mesh: groups: 2 (over x), gx: 16 (over z, y, core).
Axes of the slice: x: 2, y: 2, z: 4, core: 2. Of those that a mesh axis runs over, the one named last changes fastest.
Arguments:
- cotangent: float32 [4, 8, 8, 8, 16384], P(None, None, None, None, ('groups', 'gx')), parts along dimension 4, may hold values from -6 to 6
- base_velocity: float32 [3, 8, 8, 8, 16384], P(None, None, None, None, ('groups', 'gx')), parts along dimension 4, may hold values from -12 to 12
- viscosity: float32 [8, 8, 8, 16384], P(None, None, None, ('groups', 'gx')), parts along dimension 3, may hold values from 0.1 to 3, as said below
- elem_slot: int32 [32, 512], P(('groups', 'gx')), parts along dimension 0, may hold values from 0 to 511, each once within a row
Outputs:
- adjoint: float32 [4, 8, 8, 8, 16384], P(None, None, None, None, ('groups', 'gx')), parts along dimension 4
- dissipation: float32 [2], P('groups'), parts along dimension 0
The draws below stay inside these ranges and needn't reach their ends.
There are 2 independent parts, one for each index of `groups`. The reference program is written for one: setup_inputs(seed, part) draws one part's arguments, and reference() takes and returns one part's arrays. A program takes and returns all parts, laid end to end along the dimension named above; each array names one. Nothing has to cross between parts.
Inputs may be any that keep to these rules, and one draw needn't show every extreme that they name: viscosity is positive.
All inputs are finite; a program needn't handle non-finite values.
Results may differ from the reference program's by a relative error of at most 0.0001.
Values sent between devices are 32-bit elements; how exact they have to be, the bound alone decides.
A program may use at most 448 MiB of HBM per device.

```python
import jax
import jax.numpy as jnp
from jax import lax

NP = 8
PY = 4
PZ = 2
EX = 8
EY = 8
EZ = 8
PX = 2
ELEMS = 8192
N_GX = 16


def draw_viscosity(key, part):
    key = jax.random.fold_in(key, 11)
    count = N_GX * EX * EY * EZ
    uniform_vals = jax.random.uniform(key, (8, 8, 8, count), jnp.float32)
    rates = 0.1 * jnp.exp(jnp.log(10.0) * uniform_vals)
    block_pos = (jnp.arange(count) // (EX * EY * EZ)).astype(jnp.float32)
    profile = 1.0 + 2.0 * block_pos / jnp.float32(N_GX - 1)
    return rates * profile


def shard_levels(rng, shape, cuts, low, high):
    gain = 1.0
    for axis_at, blocks in cuts:
        steps = jax.random.uniform(jax.random.fold_in(jax.random.fold_in(rng, 6), axis_at), (blocks,), jnp.float32, low / len(cuts), high / len(cuts))
        gain = gain * jnp.repeat(jnp.exp(steps), shape[axis_at] // blocks).reshape((-1,) + (1,) * (len(shape) - 1 - axis_at))
    return gain


def gaussian(own_key, dims, scale, bound, shards=(), held_as=jnp.bfloat16):
    entries = jax.random.normal(own_key, dims, jnp.float32) * scale
    if len(shards) > 0:
        entries = shard_levels(own_key, dims, shards, -0.22, 0.18) * entries
    return jnp.clip(entries, min=-bound, max=bound).astype(held_as)


def setup_inputs(seed: int = 0, part: int = 0) -> dict:
    seeds = jax.random.split(jax.random.key(seed), 5)
    part_splits = jax.random.split(jax.random.fold_in(seeds[4], part), 5)
    cotangent = gaussian(part_splits[0], (4, NP, NP, NP, ELEMS), 1.0, 6.0, ((4, 16),), jnp.float32)
    base_velocity = gaussian(part_splits[1], (3, NP, NP, NP, ELEMS), 2.0, 12.0, ((4, 16),), jnp.float32)
    viscosity = draw_viscosity(jax.random.fold_in(jax.random.fold_in(seeds[4], part), 71), part)
    elem_slot = jax.vmap(lambda own: jax.random.permutation(own, EX * EY * EZ))(jax.random.split(part_splits[3], N_GX)).reshape((N_GX, EX * EY * EZ)).astype(jnp.int32)
    return dict(cotangent=cotangent, base_velocity=base_velocity, viscosity=viscosity, elem_slot=elem_slot)


GLL_NODES = (-1.0, -0.8717401485096066, -0.5917001814331423, -0.2092992179024789, 0.2092992179024789, 0.5917001814331423, 0.8717401485096066, 1.0)


def gll_tables():
    degree = 7
    points = list(GLL_NODES)
    previous = [1.0] * 8
    current = list(points)
    for order_idx in range(1, degree):
        following = [((2 * order_idx + 1) * point * now - order_idx * before) / (order_idx + 1) for point, now, before in zip(points, current, previous)]
        previous = current
        current = following
    legendre_vals = current
    weights = [2.0 / (degree * (degree + 1) * value * value) for value in legendre_vals]
    derivative = [[0.0] * 8 for row_idx in range(8)]
    for upper_idx in range(8):
        for lower_idx in range(8):
            if upper_idx != lower_idx:
                derivative[upper_idx][lower_idx] = legendre_vals[upper_idx] / (legendre_vals[lower_idx] * (points[upper_idx] - points[lower_idx]))
    derivative[0][0] = -degree * (degree + 1) / 4.0
    derivative[7][7] = degree * (degree + 1) / 4.0
    mass_diag = [[[[weights[first] * weights[second] * weights[third]] for third in range(8)] for second in range(8)] for first in range(8)]
    return jnp.asarray(derivative, jnp.float32), jnp.asarray(mass_diag, jnp.float32)


def along(derivative, values_in, direction, transpose):
    matrix = derivative.T if transpose else derivative
    forms = ("ai,ijkn->ajkn", "bj,ijkn->ibkn", "ck,ijkn->ijcn")
    return jnp.einsum(forms[direction], matrix, values_in, precision=lax.Precision.HIGHEST)


def prepare(derivative, mass_diag, cotangent, base_velocity, viscosity):
    weighted = mass_diag * viscosity
    pressure_w = mass_diag * cotangent[3]
    fluxes = []
    divergence = jnp.zeros_like(viscosity)
    dissipation = jnp.float32(0.0)
    for component in range(3):
        scaled_cot = mass_diag * cotangent[component]
        row_list = []
        for direction in range(3):
            grad_val = along(derivative, cotangent[component], direction, False)
            dissipation = dissipation + jnp.sum(weighted * grad_val * grad_val)
            flux_term = weighted * grad_val + base_velocity[direction] * scaled_cot
            if direction == component:
                flux_term = flux_term - pressure_w
                divergence = divergence + grad_val
            row_list.append(flux_term)
        fluxes.append(row_list)
    pressure_adj = -mass_diag * divergence
    return fluxes, pressure_adj, dissipation


def planes(derivative, fluxes, pressure_adj):
    outputs = []
    for component in range(3):
        x_part = along(derivative, fluxes[component][0], 0, True)
        y_part = along(derivative, fluxes[component][1], 1, True)
        z_part = along(derivative, fluxes[component][2], 2, True)
        outputs.append(x_part + y_part + z_part)
    outputs.append(pressure_adj)
    return jnp.stack(outputs)


def pair_sum(values_in, node_axis, stride, period):
    lower_face = lax.index_in_dim(values_in, 0, node_axis, keepdims=True)
    upper_face = lax.index_in_dim(values_in, 7, node_axis, keepdims=True)
    middle = lax.slice_in_dim(values_in, 1, 7, axis=node_axis)
    count = values_in.shape[-1]
    position = jnp.arange(count - stride, dtype=jnp.int32)
    valid = ((position // stride) % period != period - 1).astype(jnp.float32)
    from_above = lower_face[..., stride:] * valid
    from_below = upper_face[..., :count - stride] * valid
    new_upper = jnp.concatenate([upper_face[..., :count - stride] + from_above, upper_face[..., count - stride:]], -1)
    new_lower = jnp.concatenate([lower_face[..., :stride], lower_face[..., stride:] + from_below], -1)
    return jnp.concatenate([new_lower, middle, new_upper], node_axis)


def reference(cotangent, base_velocity, viscosity, elem_slot):
    derivative, mass_diag = gll_tables()
    fluxes, pressure_adj, dissipation = prepare(derivative, mass_diag, cotangent, base_velocity, viscosity)
    local_adj = planes(derivative, fluxes, pressure_adj)
    size_x = EX * PX
    size_y = EY * PY
    size_z = EZ * PZ
    xs = jnp.arange(size_x, dtype=jnp.int32)[:, None, None]
    ys = jnp.arange(size_y, dtype=jnp.int32)[None, :, None]
    zs = jnp.arange(size_z, dtype=jnp.int32)[None, None, :]
    device = (xs // EX) * (PY * PZ) + (ys // EY) * PZ + zs // EZ
    position = ((xs % EX) * EY + ys % EY) * EZ + zs % EZ
    per_block = EX * EY * EZ
    order_idx = (device * per_block + elem_slot.astype(jnp.int32)[device, position]).reshape(-1).astype(jnp.int32)
    grid = local_adj[..., order_idx]
    grid = pair_sum(grid, 1, size_y * size_z, size_x)
    grid = pair_sum(grid, 2, size_z, size_y)
    grid = pair_sum(grid, 3, 1, size_z)
    assembled = jnp.zeros_like(grid).at[..., order_idx].set(grid)
    average = dissipation / jnp.float32(512.0 * ELEMS)
    return assembled, jnp.reshape(average, (1,)).astype(jnp.float32)
```

```python
import functools

import jax
import jax.numpy as jnp
import numpy as np
from jax import lax
from jax.experimental import pallas as pl
from jax.experimental.pallas import tpu as pltpu
from jax.sharding import PartitionSpec as P

PY = 4
PZ = 2
F32 = jnp.float32
BF16 = jnp.bfloat16
STRIDE = (64, 8, 1)
GROUPS = ((0, 1), (2, 3))

GLL_NODES = (
    -1.0,
    -0.8717401485096066,
    -0.5917001814331423,
    -0.2092992179024789,
    0.2092992179024789,
    0.5917001814331423,
    0.8717401485096066,
    1.0,
)


def gll_tables():
    degree = 7
    points = np.array(GLL_NODES)
    previous = np.ones(8)
    current = points.copy()
    for order_idx in range(1, degree):
        following = ((2 * order_idx + 1) * points * current - order_idx * previous) / (order_idx + 1)
        previous, current = current, following
    weights = 2.0 / (degree * (degree + 1) * current * current)
    derivative = np.zeros((8, 8))
    for a in range(8):
        for b in range(8):
            if a != b:
                derivative[a, b] = current[a] / (current[b] * (points[a] - points[b]))
    derivative[0, 0] = -degree * (degree + 1) / 4.0
    derivative[7, 7] = degree * (degree + 1) / 4.0
    return derivative, weights


DM, WEIGHTS = gll_tables()
BACK = DM.T * WEIGHTS[None, :] / WEIGHTS[:, None]


def hi_lo(matrix):
    high = np.asarray(matrix, np.float32).astype(jnp.bfloat16)
    low = (np.asarray(matrix, np.float64) - high.astype(np.float64)).astype(np.float32).astype(jnp.bfloat16)
    return high, low


def constants():
    eye = np.eye(8)
    forward = np.concatenate([np.kron(DM, eye), np.kron(eye, DM)], 0)
    high, low = hi_lo(forward)
    forward_lhs = np.concatenate([high, low, high, low], 1)
    backward = np.concatenate([np.kron(BACK, eye), np.kron(eye, BACK)], 1)
    high, low = hi_lo(backward)
    backward_lhs = np.concatenate([np.concatenate([high, high], 1), np.concatenate([low, low], 1)], 0)
    mass = (
        WEIGHTS[:, None, None, None] * WEIGHTS[None, :, None, None] * WEIGHTS[None, None, :, None]
        * np.ones((1, 1, 1, 128))
    ).astype(np.float32)
    return jnp.asarray(forward_lhs), jnp.asarray(backward_lhs), jnp.asarray(mass)


def apply_odd(table, xs):
    even = [xs[b] + xs[7 - b] for b in range(4)]
    odd = [xs[b] - xs[7 - b] for b in range(4)]
    ys = [None] * 8
    for a in range(4):
        first = None
        second = None
        for b in range(4):
            plus = float((table[a, b] + table[a, 7 - b]) / 2)
            minus = float((table[a, b] - table[a, 7 - b]) / 2)
            first = plus * even[b] if first is None else first + plus * even[b]
            second = minus * odd[b] if second is None else second + minus * odd[b]
        ys[a] = second + first
        ys[7 - a] = second - first
    return ys


def split(x):
    high = x.astype(BF16)
    low = (x - high.astype(F32)).astype(BF16)
    return high, low


def dot(a, b):
    return jnp.dot(a, b, preferred_element_type=F32)


def onehot(mask):
    return jnp.where(mask, F32(1.0), F32(0.0)).astype(BF16)


def kernel(
    n_gx, cot_hbm, vel_hbm, visc_hbm, slot_ref, fwd_ref, bwd_ref, mass_ref, out_hbm, diss_ref,
    cot, vel, visc, loc, near, pick, place, send, halo, part, total,
    in_sem, out_sem, send_sem, recv_sem, part_send, part_recv,
):
    me = lax.axis_index("gx")
    counts = (n_gx // (PY * PZ), PY, PZ)
    strides = (PY * PZ, PZ, 1)
    coords = [(me // strides[d]) % counts[d] for d in range(3)]

    def load(src, dst, at):
        copy = pltpu.make_async_copy(src, dst, in_sem.at[at])
        copy.start()
        return copy

    loads = [
        load(cot_hbm.at[0], cot.at[0], 0),
        load(visc_hbm, visc, 1),
        load(vel_hbm.at[0], vel.at[0], 2),
        load(cot_hbm.at[3], cot.at[3], 3),
        load(vel_hbm.at[1], vel.at[1], 4),
        load(vel_hbm.at[2], vel.at[2], 5),
        load(cot_hbm.at[1], cot.at[1], 6),
        load(cot_hbm.at[2], cot.at[2], 7),
    ]

    halo[...] = jnp.zeros_like(halo)
    total[...] = jnp.zeros_like(total)
    barrier = pltpu.get_barrier_semaphore()
    for off in range(1, n_gx):
        pl.semaphore_signal(
            barrier, inc=1, device_id={"gx": lax.rem(me + off, n_gx)},
            device_id_type=pl.DeviceIdType.MESH,
        )

    slots = slot_ref[...]
    where_is = onehot(lax.broadcasted_iota(jnp.int32, (512, 512), 0) == slots)
    at_row = lax.broadcasted_iota(jnp.int32, (16, 512), 1)
    at_col = lax.broadcasted_iota(jnp.int32, (512, 128), 0)

    def code_of(at, form):
        parts = []
        for piece in (at // 8, at % 8):
            value = piece.astype(F32).astype(BF16)
            parts.append(form(value))
        return 8.0 * parts[0] + parts[1]

    row = code_of(at_row, lambda v: lax.dot_general(v, where_is, (((1,), (1,)), ((), ())), preferred_element_type=F32))
    row = row[0:1].astype(jnp.int32)
    col = code_of(at_col, lambda v: dot(where_is, v)).astype(jnp.int32)[:, 0:1]
    for d in range(3):
        step = STRIDE[d]
        place_of = (row // step) % 8
        near[d, 0] = onehot(col == jnp.where(place_of < 7, row + step, -1))
        near[d, 1] = onehot(col == jnp.where(place_of > 0, row - step, -1))
        face = (row // (8 * step)) * step + row % step
        lane = lax.broadcasted_iota(jnp.int32, (1, 128), 1)
        sub = lax.broadcasted_iota(jnp.int32, (128, 512), 0)
        for side in range(2):
            edge = 7 * side
            for which in range(2):
                q = lane - 64 * which
                inside = (q >= 0) & (q < 64)
                q = jnp.where(inside, q, 0)
                code = (q // step) * (8 * step) + edge * step + q % step
                pick[d, side, which] = onehot(col == jnp.where(inside, code, -1))
                place[d, side, which] = onehot(
                    sub == jnp.where(place_of == edge, face + 64 * which, -1)
                )

    def component(c):
        if c == 0:
            for at in (0, 1, 2, 3):
                loads[at].wait()
        else:
            loads[5 + c].wait()

        @pl.loop(0, 8)
        def _(j):
            accumulated = total[...]
            for tile in range(4):
                ls = slice(128 * tile, 128 * tile + 128)
                u = [cot[c, i, j, :, ls] for i in range(8)]
                grad = apply_odd(DM, u)
                flux = []
                for i in range(8):
                    scaled = visc[i, j, :, ls] * grad[i]
                    accumulated = accumulated + mass_ref[i, j] * (scaled * grad[i])
                    term = scaled + vel[0, i, j, :, ls] * u[i]
                    if c == 0:
                        term = term - cot[3, i, j, :, ls]
                        loc[3, i, j, :, ls] = grad[i]
                    flux.append(term)
                result = apply_odd(BACK, flux)
                for i in range(8):
                    loc[c, i, j, :, ls] = result[i]
            total[...] = accumulated

        if c == 0:
            loads[4].wait()
            loads[5].wait()

        @pl.loop(0, 8)
        def _(i):
            mass = mass_ref[i].reshape(64, 128)
            mass = jnp.concatenate([mass, mass], 1)
            for half in range(2):
                ls = slice(256 * half, 256 * half + 256)

                def take(ref, *at):
                    return ref[(*at, i, slice(None), slice(None), ls)].reshape(64, 256)

                u = take(cot, c)
                high, low = split(u)
                grad = dot(fwd_ref[...], jnp.concatenate([high, high, low, low], 0))
                grads = (grad[:64], grad[64:])
                nu = take(visc)
                fluxes = []
                energy = None
                for d in (1, 2):
                    g = grads[d - 1]
                    scaled = nu * g
                    energy = scaled * g if energy is None else energy + scaled * g
                    term = scaled + take(vel, d) * u
                    if d == c:
                        term = term - take(cot, 3)
                        div = take(loc, 3) + g
                        if c == 2:
                            div = -mass * div
                        loc[3, i, :, :, ls] = div.reshape(8, 8, 256)
                    fluxes.append(term)
                energy = jnp.sum((mass * energy).reshape(8, 8, 256), 0)
                total[...] += energy[:, :128] + energy[:, 128:]
                high, low = split(jnp.concatenate(fluxes, 0))
                back = dot(bwd_ref[...], jnp.concatenate([high, low], 0))
                value = mass * (take(loc, c) + back[:64] + back[64:])
                loc[c, i, :, :, ls] = value.reshape(8, 8, 256)

    def face_at(c, d, side):
        index = [c, slice(None), slice(None), slice(None), slice(None)]
        index[1 + d] = 7 * side
        return tuple(index)

    def get_face(c, d, side):
        return loc[face_at(c, d, side)].reshape(64, 512)

    def put_face(c, d, side, value):
        loc[face_at(c, d, side)] = value.reshape(8, 8, 512)

    def exists(d, side):
        return coords[d] < counts[d] - 1 if side else coords[d] > 0

    def remote(g, d, side):
        partner = me + strides[d] if side else me - strides[d]
        return pltpu.make_async_remote_copy(
            src_ref=send.at[g, d, side],
            dst_ref=halo.at[g, d, 1 - side],
            send_sem=send_sem.at[g, d, side],
            recv_sem=recv_sem.at[g, d, 1 - side],
            device_id={"gx": partner},
            device_id_type=pl.DeviceIdType.MESH,
        )

    def start_stage(g, d):
        comps = GROUPS[g]
        faces = {}
        for side in range(2):
            message = None
            for which in range(2):
                value = get_face(comps[which], d, side)
                stacked = jnp.concatenate(split(value), 0)
                faces[side, which] = (value, stacked)
                piece = dot(stacked, pick[d, side, which])
                message = piece if message is None else message + piece
            send[g, d, side] = message[:64] + message[64:]

            @pl.when(exists(d, side))
            def _():
                remote(g, d, side).start()

        for side in range(2):
            other = jnp.concatenate([faces[1 - side, 0][1], faces[1 - side, 1][1]], 0)
            moved = dot(other, near[d, 1 - side])
            for which in range(2):
                value = faces[side, which][0]
                base = 128 * which
                value = value + (moved[base:base + 64] + moved[base + 64:base + 128])
                put_face(comps[which], d, side, value)

    def end_stage(g, d):
        comps = GROUPS[g]
        for side in range(2):
            @pl.when(exists(d, side))
            def _():
                copy = pltpu.make_async_remote_copy(
                    src_ref=send.at[g, d, side],
                    dst_ref=halo.at[g, d, side],
                    send_sem=send_sem.at[g, d, side],
                    recv_sem=recv_sem.at[g, d, side],
                    device_id={"gx": me + strides[d] if side else me - strides[d]},
                    device_id_type=pl.DeviceIdType.MESH,
                )
                copy.wait_recv()
                copy.wait_send()

            stacked = jnp.concatenate(split(halo[g, d, side]), 0)
            for which in range(2):
                moved = dot(stacked, place[d, side, which])
                c = comps[which]
                put_face(c, d, side, get_face(c, d, side) + (moved[:64] + moved[64:]))

    def store(g):
        copies = []
        for c in GROUPS[g]:
            copy = pltpu.make_async_copy(loc.at[c], out_hbm.at[c], out_sem.at[c])
            copy.start()
            copies.append(copy)
        return copies

    def part_copy(off, slot):
        return pltpu.make_async_remote_copy(
            src_ref=part.at[me],
            dst_ref=part.at[slot],
            send_sem=part_send.at[off],
            recv_sem=part_recv.at[off],
            device_id={"gx": lax.rem(me + off, n_gx)},
            device_id_type=pl.DeviceIdType.MESH,
        )

    component(0)
    component(1)
    pl.semaphore_wait(barrier, n_gx - 1)
    start_stage(0, 0)
    component(2)
    part[me] = total[...]
    for off in range(1, n_gx):
        part_copy(off, me).start()
    start_stage(1, 0)
    end_stage(0, 0)
    start_stage(0, 1)
    end_stage(1, 0)
    start_stage(1, 1)
    end_stage(0, 1)
    start_stage(0, 2)
    end_stage(1, 1)
    start_stage(1, 2)
    end_stage(0, 2)
    copies = store(0)
    for off in range(1, n_gx):
        part_copy(off, lax.rem(me + n_gx - off, n_gx)).wait_recv()
        part_copy(off, me).wait_send()
    end_stage(1, 2)
    copies += store(1)
    summed = part[0]
    for at in range(1, n_gx):
        summed = summed + part[at]
    diss_ref[0] = jnp.sum(summed) / F32(512.0 * 512.0 * n_gx)
    for copy in copies:
        copy.wait()


def shards(cotangent, base_velocity, viscosity, elem_slot):
    n_gx = lax.axis_size("gx")
    forward, backward, mass = constants()
    hbm = pl.BlockSpec(memory_space=pl.ANY)
    vmem = pl.BlockSpec(memory_space=pltpu.VMEM)
    return pl.pallas_call(
        functools.partial(kernel, n_gx),
        out_shape=(
            jax.ShapeDtypeStruct((4, 8, 8, 8, 512), F32),
            jax.ShapeDtypeStruct((1,), F32),
        ),
        in_specs=[hbm, hbm, hbm, vmem, vmem, vmem, vmem],
        out_specs=(hbm, pl.BlockSpec(memory_space=pltpu.SMEM)),
        scratch_shapes=[
            pltpu.VMEM((4, 8, 8, 8, 512), F32),
            pltpu.VMEM((3, 8, 8, 8, 512), F32),
            pltpu.VMEM((8, 8, 8, 512), F32),
            pltpu.VMEM((4, 8, 8, 8, 512), F32),
            pltpu.VMEM((3, 2, 512, 512), BF16),
            pltpu.VMEM((3, 2, 2, 512, 128), BF16),
            pltpu.VMEM((3, 2, 2, 128, 512), BF16),
            pltpu.VMEM((2, 3, 2, 64, 128), F32),
            pltpu.VMEM((2, 3, 2, 64, 128), F32),
            pltpu.VMEM((n_gx, 8, 128), F32),
            pltpu.VMEM((8, 128), F32),
            pltpu.SemaphoreType.DMA((8,)),
            pltpu.SemaphoreType.DMA((4,)),
            pltpu.SemaphoreType.DMA((2, 3, 2)),
            pltpu.SemaphoreType.DMA((2, 3, 2)),
            pltpu.SemaphoreType.DMA((n_gx,)),
            pltpu.SemaphoreType.DMA((n_gx,)),
        ],
        compiler_params=pltpu.CompilerParams(
            collective_id=0, has_side_effects=True, vmem_limit_bytes=48 * 1024 * 1024
        ),
        cost_estimate=pl.CostEstimate(flops=6 * 10**9, bytes_accessed=12 * 2**20, transcendentals=0),
    )(cotangent, base_velocity, viscosity, elem_slot, forward, backward, mass)


def solution(mesh):
    in_specs = (
        P(None, None, None, None, ("groups", "gx")),
        P(None, None, None, None, ("groups", "gx")),
        P(None, None, None, ("groups", "gx")),
        P(("groups", "gx"), None),
    )
    out_specs = (P(None, None, None, None, ("groups", "gx")), P("groups"))
    return jax.shard_map(shards, mesh=mesh, in_specs=in_specs, out_specs=out_specs, check_vma=False)
```

```python
import functools

import jax
import jax.numpy as jnp
import numpy as np
from jax import lax
from jax.experimental import pallas as pl
from jax.experimental.pallas import tpu as pltpu
from jax.sharding import PartitionSpec as P

PY = 4
PZ = 2
F32 = jnp.float32
BF16 = jnp.bfloat16
STRIDE = (64, 8, 1)
GROUPS = ((0, 1), (2, 3))

GLL_NODES = (
    -1.0,
    -0.8717401485096066,
    -0.5917001814331423,
    -0.2092992179024789,
    0.2092992179024789,
    0.5917001814331423,
    0.8717401485096066,
    1.0,
)


def gll_tables():
    degree = 7
    points = np.array(GLL_NODES)
    previous = np.ones(8)
    current = points.copy()
    for order_idx in range(1, degree):
        following = ((2 * order_idx + 1) * points * current - order_idx * previous) / (order_idx + 1)
        previous, current = current, following
    weights = 2.0 / (degree * (degree + 1) * current * current)
    derivative = np.zeros((8, 8))
    for a in range(8):
        for b in range(8):
            if a != b:
                derivative[a, b] = current[a] / (current[b] * (points[a] - points[b]))
    derivative[0, 0] = -degree * (degree + 1) / 4.0
    derivative[7, 7] = degree * (degree + 1) / 4.0
    return derivative, weights


DM, WEIGHTS = gll_tables()
BACK = DM.T * WEIGHTS[None, :] / WEIGHTS[:, None]


def hi_lo(matrix):
    high = np.asarray(matrix, np.float32).astype(jnp.bfloat16)
    low = (np.asarray(matrix, np.float64) - high.astype(np.float64)).astype(np.float32).astype(jnp.bfloat16)
    return high, low


def constants():
    eye = np.eye(8)
    forward = np.concatenate([np.kron(DM, eye), np.kron(eye, DM)], 0)
    high, low = hi_lo(forward)
    forward_lhs = np.concatenate([high, low, high, low], 1)
    backward = np.concatenate([np.kron(BACK, eye), np.kron(eye, BACK)], 1)
    high, low = hi_lo(backward)
    backward_lhs = np.concatenate([np.concatenate([high, high], 1), np.concatenate([low, low], 1)], 0)
    mass = (
        WEIGHTS[:, None, None, None] * WEIGHTS[None, :, None, None] * WEIGHTS[None, None, :, None]
        * np.ones((1, 1, 1, 128))
    ).astype(np.float32)
    return jnp.asarray(forward_lhs), jnp.asarray(backward_lhs), jnp.asarray(mass)


def apply_odd(table, xs):
    even = [xs[b] + xs[7 - b] for b in range(4)]
    odd = [xs[b] - xs[7 - b] for b in range(4)]
    ys = [None] * 8
    for a in range(4):
        first = None
        second = None
        for b in range(4):
            plus = float((table[a, b] + table[a, 7 - b]) / 2)
            minus = float((table[a, b] - table[a, 7 - b]) / 2)
            first = plus * even[b] if first is None else first + plus * even[b]
            second = minus * odd[b] if second is None else second + minus * odd[b]
        ys[a] = second + first
        ys[7 - a] = second - first
    return ys


def split(x):
    high = x.astype(BF16)
    low = (x - high.astype(F32)).astype(BF16)
    return high, low


def dot(a, b):
    return jnp.dot(a, b, preferred_element_type=F32)


def onehot(mask):
    return jnp.where(mask, F32(1.0), F32(0.0)).astype(BF16)


def kernel(
    n_gx, cot_hbm, vel_hbm, visc_hbm, slot_ref, fwd_hbm, bwd_hbm, mass_hbm, out_hbm, diss_ref,
    fwd_ref, bwd_ref, mass_ref, cot, vel, visc, loc, near, pick, place, send, halo, part, other, total,
    in_sem, out_sem, send_sem, recv_sem, part_send, part_recv,
):
    me = lax.axis_index("gx")
    counts = (n_gx // (PY * PZ), PY, PZ)
    strides = (PY * PZ, PZ, 1)
    coords = [(me // strides[d]) % counts[d] for d in range(3)]

    bits = (n_gx - 1).bit_length()

    def exists(d, side):
        return coords[d] < counts[d] - 1 if side else coords[d] > 0

    def load(src, dst, at):
        copy = pltpu.make_async_copy(src, dst, in_sem.at[at])
        copy.start()
        return copy

    tables = [
        load(mass_hbm, mass_ref, 8),
        load(fwd_hbm, fwd_ref, 9),
        load(bwd_hbm, bwd_ref, 10),
    ]
    loads = [
        load(cot_hbm.at[0], cot.at[0], 0),
        load(visc_hbm, visc, 1),
        load(vel_hbm.at[0], vel.at[0], 2),
        load(cot_hbm.at[3], cot.at[3], 3),
        load(vel_hbm.at[1], vel.at[1], 4),
        load(vel_hbm.at[2], vel.at[2], 5),
        load(cot_hbm.at[1], cot.at[1], 6),
        load(cot_hbm.at[2], cot.at[2], 7),
    ]

    halo[...] = jnp.zeros_like(halo)
    total[...] = jnp.zeros_like(total)
    barrier = pltpu.get_barrier_semaphore()

    def greet(partner):
        pl.semaphore_signal(
            barrier, inc=1, device_id={"gx": partner}, device_id_type=pl.DeviceIdType.MESH
        )

    for bit in range(bits):
        greet(me ^ (1 << bit))
    expected = bits
    for d in range(3):
        for side in range(2):
            there = exists(d, side)
            expected = expected + there.astype(jnp.int32)

            @pl.when(there)
            def _():
                greet(me + strides[d] if side else me - strides[d])

    slots = slot_ref[...]
    where_is = onehot(lax.broadcasted_iota(jnp.int32, (512, 512), 0) == slots)
    at_row = lax.broadcasted_iota(jnp.int32, (16, 512), 1)
    at_col = lax.broadcasted_iota(jnp.int32, (512, 128), 0)

    def code_of(at, form):
        parts = []
        for piece in (at // 8, at % 8):
            value = piece.astype(F32).astype(BF16)
            parts.append(form(value))
        return 8.0 * parts[0] + parts[1]

    row = code_of(at_row, lambda v: lax.dot_general(v, where_is, (((1,), (1,)), ((), ())), preferred_element_type=F32))
    row = row[0:1].astype(jnp.int32)
    col = code_of(at_col, lambda v: dot(where_is, v)).astype(jnp.int32)[:, 0:1]
    for d in range(3):
        step = STRIDE[d]
        place_of = (row // step) % 8
        near[d, 0] = onehot(col == jnp.where(place_of < 7, row + step, -1))
        near[d, 1] = onehot(col == jnp.where(place_of > 0, row - step, -1))
        face = (row // (8 * step)) * step + row % step
        lane = lax.broadcasted_iota(jnp.int32, (1, 128), 1)
        sub = lax.broadcasted_iota(jnp.int32, (128, 512), 0)
        for side in range(2):
            edge = 7 * side
            for which in range(2):
                q = lane - 64 * which
                inside = (q >= 0) & (q < 64)
                q = jnp.where(inside, q, 0)
                code = (q // step) * (8 * step) + edge * step + q % step
                pick[d, side, which] = onehot(col == jnp.where(inside, code, -1))
                place[d, side, which] = onehot(
                    sub == jnp.where(place_of == edge, face + 64 * which, -1)
                )

    def component(c):
        if c == 0:
            tables[0].wait()
            for at in (0, 1, 2, 3):
                loads[at].wait()
        else:
            loads[5 + c].wait()

        @pl.loop(0, 8)
        def _(j):
            accumulated = total[...]
            for tile in range(4):
                ls = slice(128 * tile, 128 * tile + 128)
                u = [cot[c, i, j, :, ls] for i in range(8)]
                grad = apply_odd(DM, u)
                flux = []
                for i in range(8):
                    scaled = visc[i, j, :, ls] * grad[i]
                    accumulated = accumulated + mass_ref[i, j] * (scaled * grad[i])
                    term = scaled + vel[0, i, j, :, ls] * u[i]
                    if c == 0:
                        term = term - cot[3, i, j, :, ls]
                        loc[3, i, j, :, ls] = grad[i]
                    flux.append(term)
                result = apply_odd(BACK, flux)
                for i in range(8):
                    loc[c, i, j, :, ls] = result[i]
            total[...] = accumulated

        if c == 0:
            loads[4].wait()
            loads[5].wait()
            tables[1].wait()
            tables[2].wait()

        @pl.loop(0, 8, step=4)
        def _(first):
            chains = [(first + more, slice(256 * half, 256 * half + 256)) for more in range(4) for half in range(2)]

            def take(ref, chain, *at):
                i, ls = chain
                return ref[(*at, i, slice(None), slice(None), ls)].reshape(64, 256)

            grads = []
            for chain in chains:
                high, low = split(take(cot, chain, c))
                grads.append(dot(fwd_ref[...], jnp.concatenate([high, high, low, low], 0)))
            masses = []
            energies = []
            divs = []
            stacks = []
            for chain, grad in zip(chains, grads):
                mass = mass_ref[chain[0]].reshape(64, 128)
                mass = jnp.concatenate([mass, mass], 1)
                u = take(cot, chain, c)
                nu = take(visc, chain)
                fluxes = []
                energy = None
                for d in (1, 2):
                    g = grad[64 * (d - 1):64 * d]
                    scaled = nu * g
                    energy = scaled * g if energy is None else energy + scaled * g
                    term = scaled + take(vel, chain, d) * u
                    if d == c:
                        term = term - take(cot, chain, 3)
                        div = take(loc, chain, 3) + g
                        divs.append(-mass * div if c == 2 else div)
                    fluxes.append(term)
                energy = jnp.sum((mass * energy).reshape(8, 8, 256), 0)
                energies.append(energy[:, :128] + energy[:, 128:])
                masses.append(mass)
                high, low = split(jnp.concatenate(fluxes, 0))
                stacks.append(jnp.concatenate([high, low], 0))
            backs = [dot(bwd_ref[...], stack) for stack in stacks]
            values = [
                mass * (take(loc, chain, c) + back[:64] + back[64:])
                for chain, mass, back in zip(chains, masses, backs)
            ]
            total[...] += sum(energies[1:], energies[0])
            for at, (i, ls) in enumerate(chains):
                loc[c, i, :, :, ls] = values[at].reshape(8, 8, 256)
                if divs:
                    loc[3, i, :, :, ls] = divs[at].reshape(8, 8, 256)

    def face_at(c, d, side):
        index = [c, slice(None), slice(None), slice(None), slice(None)]
        index[1 + d] = 7 * side
        return tuple(index)

    def get_face(c, d, side):
        return loc[face_at(c, d, side)].reshape(64, 512)

    def put_face(c, d, side, value):
        loc[face_at(c, d, side)] = value.reshape(8, 8, 512)

    def remote(g, d, side):
        partner = me + strides[d] if side else me - strides[d]
        return pltpu.make_async_remote_copy(
            src_ref=send.at[g, d, side],
            dst_ref=halo.at[g, d, 1 - side],
            send_sem=send_sem.at[g, d, side],
            recv_sem=recv_sem.at[g, d, 1 - side],
            device_id={"gx": partner},
            device_id_type=pl.DeviceIdType.MESH,
        )

    def start_stage(g, d):
        comps = GROUPS[g]
        faces = {}
        for side in range(2):
            message = None
            for which in range(2):
                value = get_face(comps[which], d, side)
                stacked = jnp.concatenate(split(value), 0)
                faces[side, which] = (value, stacked)
                piece = dot(stacked, pick[d, side, which])
                message = piece if message is None else message + piece
            send[g, d, side] = message[:64] + message[64:]

            @pl.when(exists(d, side))
            def _():
                remote(g, d, side).start()

        for side in range(2):
            across = jnp.concatenate([faces[1 - side, 0][1], faces[1 - side, 1][1]], 0)
            moved = dot(across, near[d, 1 - side])
            for which in range(2):
                value = faces[side, which][0]
                base = 128 * which
                value = value + (moved[base:base + 64] + moved[base + 64:base + 128])
                put_face(comps[which], d, side, value)

    def end_stage(g, d):
        comps = GROUPS[g]
        for side in range(2):
            @pl.when(exists(d, side))
            def _():
                copy = pltpu.make_async_remote_copy(
                    src_ref=send.at[g, d, side],
                    dst_ref=halo.at[g, d, side],
                    send_sem=send_sem.at[g, d, side],
                    recv_sem=recv_sem.at[g, d, side],
                    device_id={"gx": me + strides[d] if side else me - strides[d]},
                    device_id_type=pl.DeviceIdType.MESH,
                )
                copy.wait_recv()
                copy.wait_send()

            stacked = jnp.concatenate(split(halo[g, d, side]), 0)
            for which in range(2):
                moved = dot(stacked, place[d, side, which])
                c = comps[which]
                put_face(c, d, side, get_face(c, d, side) + (moved[:64] + moved[64:]))

    def store(g):
        copies = []
        for c in GROUPS[g]:
            copy = pltpu.make_async_copy(loc.at[c], out_hbm.at[c], out_sem.at[c])
            copy.start()
            copies.append(copy)
        return copies

    def part_copy(bit):
        return pltpu.make_async_remote_copy(
            src_ref=part.at[bit],
            dst_ref=other.at[bit],
            send_sem=part_send.at[bit],
            recv_sem=part_recv.at[bit],
            device_id={"gx": me ^ (1 << bit)},
            device_id_type=pl.DeviceIdType.MESH,
        )

    def reduce_bit(bit):
        part_copy(bit).wait_recv()
        part[bit + 1] = part[bit] + other[bit]
        if bit + 1 < bits:
            part_copy(bit + 1).start()

    component(0)
    component(1)
    pl.semaphore_wait(barrier, expected)
    start_stage(0, 0)
    component(2)
    part[0] = total[...]
    part_copy(0).start()
    start_stage(1, 0)
    end_stage(0, 0)
    reduce_bit(0)
    start_stage(0, 1)
    end_stage(1, 0)
    start_stage(1, 1)
    reduce_bit(1)
    end_stage(0, 1)
    start_stage(0, 2)
    end_stage(1, 1)
    reduce_bit(2)
    start_stage(1, 2)
    end_stage(0, 2)
    copies = store(0)
    end_stage(1, 2)
    copies += store(1)
    for bit in range(3, bits):
        reduce_bit(bit)
    diss_ref[0] = jnp.sum(part[bits]) / F32(512.0 * 512.0 * n_gx)
    for bit in range(bits):
        part_copy(bit).wait_send()
    for copy in copies:
        copy.wait()


def hand_over_kernel(src, dst, held, in_sem, out_sem):
    def incoming(at):
        return pltpu.make_async_copy(src.at[at // 2, pl.ds(4 * (at % 2), 4)], held.at[at], in_sem.at[at])

    def outgoing(at):
        return pltpu.make_async_copy(held.at[at], dst.at[at // 2, pl.ds(4 * (at % 2), 4)], out_sem.at[at])

    for at in range(8):
        incoming(at).start()
    for at in range(8):
        incoming(at).wait()
        outgoing(at).start()
    for at in range(8):
        outgoing(at).wait()


def hand_over(value):
    return pl.pallas_call(
        hand_over_kernel,
        out_shape=jax.ShapeDtypeStruct(value.shape, F32),
        in_specs=[pl.BlockSpec(memory_space=pl.ANY)],
        out_specs=pl.BlockSpec(memory_space=pl.ANY),
        scratch_shapes=[
            pltpu.VMEM((8, 4, 8, 8, 512), F32),
            pltpu.SemaphoreType.DMA((8,)),
            pltpu.SemaphoreType.DMA((8,)),
        ],
        compiler_params=pltpu.CompilerParams(vmem_limit_bytes=60 * 1024 * 1024),
    )(value)


def shards(cotangent, base_velocity, viscosity, elem_slot):
    n_gx = lax.axis_size("gx")
    bits = (n_gx - 1).bit_length()
    forward, backward, mass = constants()
    hbm = pl.BlockSpec(memory_space=pl.ANY)
    vmem = pl.BlockSpec(memory_space=pltpu.VMEM)
    assembled, average = pl.pallas_call(
        functools.partial(kernel, n_gx),
        out_shape=(
            jax.ShapeDtypeStruct((4, 8, 8, 8, 512), F32),
            jax.ShapeDtypeStruct((1,), F32),
        ),
        in_specs=[hbm, hbm, hbm, vmem, hbm, hbm, hbm],
        out_specs=(hbm, pl.BlockSpec(memory_space=pltpu.SMEM)),
        scratch_shapes=[
            pltpu.VMEM((128, 256), BF16),
            pltpu.VMEM((128, 256), BF16),
            pltpu.VMEM((8, 8, 8, 128), F32),
            pltpu.VMEM((4, 8, 8, 8, 512), F32),
            pltpu.VMEM((3, 8, 8, 8, 512), F32),
            pltpu.VMEM((8, 8, 8, 512), F32),
            pltpu.VMEM((4, 8, 8, 8, 512), F32),
            pltpu.VMEM((3, 2, 512, 512), BF16),
            pltpu.VMEM((3, 2, 2, 512, 128), BF16),
            pltpu.VMEM((3, 2, 2, 128, 512), BF16),
            pltpu.VMEM((2, 3, 2, 64, 128), F32),
            pltpu.VMEM((2, 3, 2, 64, 128), F32),
            pltpu.VMEM((bits + 1, 8, 128), F32),
            pltpu.VMEM((bits, 8, 128), F32),
            pltpu.VMEM((8, 128), F32),
            pltpu.SemaphoreType.DMA((11,)),
            pltpu.SemaphoreType.DMA((4,)),
            pltpu.SemaphoreType.DMA((2, 3, 2)),
            pltpu.SemaphoreType.DMA((2, 3, 2)),
            pltpu.SemaphoreType.DMA((bits,)),
            pltpu.SemaphoreType.DMA((bits,)),
        ],
        compiler_params=pltpu.CompilerParams(
            collective_id=0, has_side_effects=True, vmem_limit_bytes=60 * 1024 * 1024
        ),
        cost_estimate=pl.CostEstimate(flops=6 * 10**9, bytes_accessed=12 * 2**20, transcendentals=0),
    )(cotangent, base_velocity, viscosity, elem_slot, forward, backward, mass)
    return hand_over(assembled), average


def solution(mesh):
    in_specs = (
        P(None, None, None, None, ("groups", "gx")),
        P(None, None, None, None, ("groups", "gx")),
        P(None, None, None, ("groups", "gx")),
        P(("groups", "gx"), None),
    )
    out_specs = (P(None, None, None, None, ("groups", "gx")), P("groups"))
    return jax.shard_map(shards, mesh=mesh, in_specs=in_specs, out_specs=out_specs, check_vma=False)
```

```python
import functools

import jax
import jax.numpy as jnp
import numpy as np
from jax import lax
from jax.experimental import pallas as pl
from jax.experimental.pallas import tpu as pltpu
from jax.sharding import PartitionSpec as P

PY = 4
PZ = 2
F32 = jnp.float32
BF16 = jnp.bfloat16
STRIDE = (64, 8, 1)
GROUPS = ((0, 1), (2, 3))

GLL_NODES = (
    -1.0,
    -0.8717401485096066,
    -0.5917001814331423,
    -0.2092992179024789,
    0.2092992179024789,
    0.5917001814331423,
    0.8717401485096066,
    1.0,
)


def gll_tables():
    degree = 7
    points = np.array(GLL_NODES)
    previous = np.ones(8)
    current = points.copy()
    for order_idx in range(1, degree):
        following = ((2 * order_idx + 1) * points * current - order_idx * previous) / (order_idx + 1)
        previous, current = current, following
    weights = 2.0 / (degree * (degree + 1) * current * current)
    derivative = np.zeros((8, 8))
    for a in range(8):
        for b in range(8):
            if a != b:
                derivative[a, b] = current[a] / (current[b] * (points[a] - points[b]))
    derivative[0, 0] = -degree * (degree + 1) / 4.0
    derivative[7, 7] = degree * (degree + 1) / 4.0
    return derivative, weights


DM, WEIGHTS = gll_tables()
BACK = DM.T * WEIGHTS[None, :] / WEIGHTS[:, None]


def hi_lo(matrix):
    high = np.asarray(matrix, np.float32).astype(jnp.bfloat16)
    low = (np.asarray(matrix, np.float64) - high.astype(np.float64)).astype(np.float32).astype(jnp.bfloat16)
    return high, low


def constants():
    eye = np.eye(8)
    forward = np.concatenate([np.kron(DM, eye), np.kron(eye, DM)], 0)
    high, low = hi_lo(forward)
    forward_lhs = np.concatenate([high, low, high, low], 1)
    backward = np.concatenate([np.kron(BACK, eye), np.kron(eye, BACK)], 1)
    high, low = hi_lo(backward)
    backward_lhs = np.concatenate([np.concatenate([high, high], 1), np.concatenate([low, low], 1)], 0)
    mass = (
        WEIGHTS[:, None, None, None] * WEIGHTS[None, :, None, None] * WEIGHTS[None, None, :, None]
        * np.ones((1, 1, 1, 128))
    ).astype(np.float32)
    return jnp.asarray(forward_lhs), jnp.asarray(backward_lhs), jnp.asarray(mass)


def apply_odd(table, xs):
    even = [xs[b] + xs[7 - b] for b in range(4)]
    odd = [xs[b] - xs[7 - b] for b in range(4)]
    ys = [None] * 8
    for a in range(4):
        first = None
        second = None
        for b in range(4):
            plus = float((table[a, b] + table[a, 7 - b]) / 2)
            minus = float((table[a, b] - table[a, 7 - b]) / 2)
            first = plus * even[b] if first is None else first + plus * even[b]
            second = minus * odd[b] if second is None else second + minus * odd[b]
        ys[a] = second + first
        ys[7 - a] = second - first
    return ys


def split(x):
    high = x.astype(BF16)
    low = (x - high.astype(F32)).astype(BF16)
    return high, low


def dot(a, b):
    return jnp.dot(a, b, preferred_element_type=F32)


def onehot(mask):
    return jnp.where(mask, F32(1.0), F32(0.0)).astype(BF16)


def kernel(
    n_gx, cot_hbm, vel_hbm, visc_hbm, slot_ref, fwd_hbm, bwd_hbm, mass_hbm, out_hbm, diss_ref,
    fwd_ref, bwd_ref, mass_ref, cot, vel, visc, loc, near, pick, place, send, halo, part, other, total,
    in_sem, out_sem, send_sem, recv_sem, part_send, part_recv,
):
    me = lax.axis_index("gx")
    counts = (n_gx // (PY * PZ), PY, PZ)
    strides = (PY * PZ, PZ, 1)
    coords = [(me // strides[d]) % counts[d] for d in range(3)]

    bits = (n_gx - 1).bit_length()

    def exists(d, side):
        return coords[d] < counts[d] - 1 if side else coords[d] > 0

    def load(src, dst, at):
        copy = pltpu.make_async_copy(src, dst, in_sem.at[at])
        copy.start()
        return copy

    tables = [
        load(mass_hbm, mass_ref, 8),
        load(fwd_hbm, fwd_ref, 9),
        load(bwd_hbm, bwd_ref, 10),
    ]
    loads = [
        load(cot_hbm.at[0], cot.at[0], 0),
        load(visc_hbm, visc, 1),
        load(vel_hbm.at[0], vel.at[0], 2),
        load(cot_hbm.at[3], cot.at[3], 3),
        load(vel_hbm.at[1], vel.at[1], 4),
        load(vel_hbm.at[2], vel.at[2], 5),
        load(cot_hbm.at[1], cot.at[1], 6),
        load(cot_hbm.at[2], cot.at[2], 7),
    ]

    halo[...] = jnp.zeros_like(halo)
    total[...] = jnp.zeros_like(total)
    barrier = pltpu.get_barrier_semaphore()

    def greet(partner):
        pl.semaphore_signal(
            barrier, inc=1, device_id={"gx": partner}, device_id_type=pl.DeviceIdType.MESH
        )

    for bit in range(bits):
        greet(me ^ (1 << bit))
    expected = bits
    for d in range(3):
        for side in range(2):
            there = exists(d, side)
            expected = expected + there.astype(jnp.int32)

            @pl.when(there)
            def _():
                greet(me + strides[d] if side else me - strides[d])

    slots = slot_ref[...]
    where_is = onehot(lax.broadcasted_iota(jnp.int32, (512, 512), 0) == slots)
    at_row = lax.broadcasted_iota(jnp.int32, (16, 512), 1)
    at_col = lax.broadcasted_iota(jnp.int32, (512, 128), 0)

    def code_of(at, form):
        parts = []
        for piece in (at // 8, at % 8):
            value = piece.astype(F32).astype(BF16)
            parts.append(form(value))
        return 8.0 * parts[0] + parts[1]

    row = code_of(at_row, lambda v: lax.dot_general(v, where_is, (((1,), (1,)), ((), ())), preferred_element_type=F32))
    row = row[0:1].astype(jnp.int32)
    col = code_of(at_col, lambda v: dot(where_is, v)).astype(jnp.int32)[:, 0:1]
    for d in range(3):
        step = STRIDE[d]
        place_of = (row // step) % 8
        near[d, 0] = onehot(col == jnp.where(place_of < 7, row + step, -1))
        near[d, 1] = onehot(col == jnp.where(place_of > 0, row - step, -1))
        face = (row // (8 * step)) * step + row % step
        lane = lax.broadcasted_iota(jnp.int32, (1, 128), 1)
        sub = lax.broadcasted_iota(jnp.int32, (128, 512), 0)
        for side in range(2):
            edge = 7 * side
            for which in range(2):
                q = lane - 64 * which
                inside = (q >= 0) & (q < 64)
                q = jnp.where(inside, q, 0)
                code = (q // step) * (8 * step) + edge * step + q % step
                pick[d, side, which] = onehot(col == jnp.where(inside, code, -1))
                place[d, side, which] = onehot(
                    sub == jnp.where(place_of == edge, face + 64 * which, -1)
                )

    def component(c):
        if c == 0:
            tables[0].wait()
            for at in (0, 1, 2, 3):
                loads[at].wait()
        else:
            loads[5 + c].wait()

        @pl.loop(0, 8)
        def _(j):
            accumulated = total[...]
            for tile in range(4):
                ls = slice(128 * tile, 128 * tile + 128)
                u = [cot[c, i, j, :, ls] for i in range(8)]
                grad = apply_odd(DM, u)
                flux = []
                for i in range(8):
                    scaled = visc[i, j, :, ls] * grad[i]
                    accumulated = accumulated + mass_ref[i, j] * (scaled * grad[i])
                    term = scaled + vel[0, i, j, :, ls] * u[i]
                    if c == 0:
                        term = term - cot[3, i, j, :, ls]
                        loc[3, i, j, :, ls] = grad[i]
                    flux.append(term)
                result = apply_odd(BACK, flux)
                for i in range(8):
                    loc[c, i, j, :, ls] = result[i]
            total[...] = accumulated

        if c == 0:
            loads[4].wait()
            loads[5].wait()
            tables[1].wait()
            tables[2].wait()

        @pl.loop(0, 8, step=8)
        def _(first):
            chains = [(first + more, slice(256 * half, 256 * half + 256)) for more in range(8) for half in range(2)]

            def take(ref, chain, *at):
                i, ls = chain
                return ref[(*at, i, slice(None), slice(None), ls)].reshape(64, 256)

            grads = []
            for chain in chains:
                high, low = split(take(cot, chain, c))
                grads.append(dot(fwd_ref[...], jnp.concatenate([high, high, low, low], 0)))
            masses = []
            energies = []
            divs = []
            stacks = []
            for chain, grad in zip(chains, grads):
                mass = mass_ref[chain[0]].reshape(64, 128)
                mass = jnp.concatenate([mass, mass], 1)
                u = take(cot, chain, c)
                nu = take(visc, chain)
                fluxes = []
                energy = None
                for d in (1, 2):
                    g = grad[64 * (d - 1):64 * d]
                    scaled = nu * g
                    energy = scaled * g if energy is None else energy + scaled * g
                    term = scaled + take(vel, chain, d) * u
                    if d == c:
                        term = term - take(cot, chain, 3)
                        div = take(loc, chain, 3) + g
                        divs.append(-mass * div if c == 2 else div)
                    fluxes.append(term)
                energy = jnp.sum((mass * energy).reshape(8, 8, 256), 0)
                energies.append(energy[:, :128] + energy[:, 128:])
                masses.append(mass)
                high, low = split(jnp.concatenate(fluxes, 0))
                stacks.append(jnp.concatenate([high, low], 0))
            backs = [dot(bwd_ref[...], stack) for stack in stacks]
            values = [
                mass * (take(loc, chain, c) + back[:64] + back[64:])
                for chain, mass, back in zip(chains, masses, backs)
            ]
            total[...] += sum(energies[1:], energies[0])
            for at, (i, ls) in enumerate(chains):
                loc[c, i, :, :, ls] = values[at].reshape(8, 8, 256)
                if divs:
                    loc[3, i, :, :, ls] = divs[at].reshape(8, 8, 256)

    def face_at(c, d, side):
        index = [c, slice(None), slice(None), slice(None), slice(None)]
        index[1 + d] = 7 * side
        return tuple(index)

    def get_face(c, d, side):
        return loc[face_at(c, d, side)].reshape(64, 512)

    def put_face(c, d, side, value):
        loc[face_at(c, d, side)] = value.reshape(8, 8, 512)

    def remote(g, d, side):
        partner = me + strides[d] if side else me - strides[d]
        return pltpu.make_async_remote_copy(
            src_ref=send.at[g, d, side],
            dst_ref=halo.at[g, d, 1 - side],
            send_sem=send_sem.at[g, d, side],
            recv_sem=recv_sem.at[g, d, 1 - side],
            device_id={"gx": partner},
            device_id_type=pl.DeviceIdType.MESH,
        )

    def start_stage(g, d):
        comps = GROUPS[g]
        faces = {}
        for side in range(2):
            message = None
            for which in range(2):
                value = get_face(comps[which], d, side)
                stacked = jnp.concatenate(split(value), 0)
                faces[side, which] = (value, stacked)
                piece = dot(stacked, pick[d, side, which])
                message = piece if message is None else message + piece
            send[g, d, side] = message[:64] + message[64:]

            @pl.when(exists(d, side))
            def _():
                remote(g, d, side).start()

        for side in range(2):
            across = jnp.concatenate([faces[1 - side, 0][1], faces[1 - side, 1][1]], 0)
            moved = dot(across, near[d, 1 - side])
            for which in range(2):
                value = faces[side, which][0]
                base = 128 * which
                value = value + (moved[base:base + 64] + moved[base + 64:base + 128])
                put_face(comps[which], d, side, value)

    def end_stage(g, d):
        comps = GROUPS[g]
        for side in range(2):
            @pl.when(exists(d, side))
            def _():
                copy = pltpu.make_async_remote_copy(
                    src_ref=send.at[g, d, side],
                    dst_ref=halo.at[g, d, side],
                    send_sem=send_sem.at[g, d, side],
                    recv_sem=recv_sem.at[g, d, side],
                    device_id={"gx": me + strides[d] if side else me - strides[d]},
                    device_id_type=pl.DeviceIdType.MESH,
                )
                copy.wait_recv()
                copy.wait_send()

            stacked = jnp.concatenate(split(halo[g, d, side]), 0)
            for which in range(2):
                moved = dot(stacked, place[d, side, which])
                c = comps[which]
                put_face(c, d, side, get_face(c, d, side) + (moved[:64] + moved[64:]))

    def store(g):
        copies = []
        for c in GROUPS[g]:
            copy = pltpu.make_async_copy(loc.at[c], out_hbm.at[c], out_sem.at[c])
            copy.start()
            copies.append(copy)
        return copies

    def part_copy(bit):
        return pltpu.make_async_remote_copy(
            src_ref=part.at[bit],
            dst_ref=other.at[bit],
            send_sem=part_send.at[bit],
            recv_sem=part_recv.at[bit],
            device_id={"gx": me ^ (1 << bit)},
            device_id_type=pl.DeviceIdType.MESH,
        )

    def reduce_bit(bit):
        part_copy(bit).wait_recv()
        part[bit + 1] = part[bit] + other[bit]
        if bit + 1 < bits:
            part_copy(bit + 1).start()

    component(0)
    component(1)
    pl.semaphore_wait(barrier, expected)
    start_stage(0, 0)
    component(2)
    part[0] = total[...]
    part_copy(0).start()
    start_stage(1, 0)
    end_stage(0, 0)
    reduce_bit(0)
    start_stage(0, 1)
    end_stage(1, 0)
    start_stage(1, 1)
    reduce_bit(1)
    end_stage(0, 1)
    start_stage(0, 2)
    end_stage(1, 1)
    reduce_bit(2)
    start_stage(1, 2)
    end_stage(0, 2)
    copies = store(0)
    end_stage(1, 2)
    copies += store(1)
    for bit in range(3, bits):
        reduce_bit(bit)
    diss_ref[0] = jnp.sum(part[bits]) / F32(512.0 * 512.0 * n_gx)
    for bit in range(bits):
        part_copy(bit).wait_send()
    for copy in copies:
        copy.wait()


def hand_over_kernel(src, dst, held, in_sem, out_sem):
    def incoming(at):
        return pltpu.make_async_copy(src.at[at // 2, pl.ds(4 * (at % 2), 4)], held.at[at], in_sem.at[at])

    def outgoing(at):
        return pltpu.make_async_copy(held.at[at], dst.at[at // 2, pl.ds(4 * (at % 2), 4)], out_sem.at[at])

    for at in range(8):
        incoming(at).start()
    for at in range(8):
        incoming(at).wait()
        outgoing(at).start()
    for at in range(8):
        outgoing(at).wait()


def hand_over(value):
    return pl.pallas_call(
        hand_over_kernel,
        out_shape=jax.ShapeDtypeStruct(value.shape, F32),
        in_specs=[pl.BlockSpec(memory_space=pl.ANY)],
        out_specs=pl.BlockSpec(memory_space=pl.ANY),
        scratch_shapes=[
            pltpu.VMEM((8, 4, 8, 8, 512), F32),
            pltpu.SemaphoreType.DMA((8,)),
            pltpu.SemaphoreType.DMA((8,)),
        ],
        compiler_params=pltpu.CompilerParams(vmem_limit_bytes=60 * 1024 * 1024),
    )(value)


def shards(cotangent, base_velocity, viscosity, elem_slot):
    n_gx = lax.axis_size("gx")
    bits = (n_gx - 1).bit_length()
    forward, backward, mass = constants()
    hbm = pl.BlockSpec(memory_space=pl.ANY)
    vmem = pl.BlockSpec(memory_space=pltpu.VMEM)
    assembled, average = pl.pallas_call(
        functools.partial(kernel, n_gx),
        out_shape=(
            jax.ShapeDtypeStruct((4, 8, 8, 8, 512), F32),
            jax.ShapeDtypeStruct((1,), F32),
        ),
        in_specs=[hbm, hbm, hbm, vmem, hbm, hbm, hbm],
        out_specs=(hbm, pl.BlockSpec(memory_space=pltpu.SMEM)),
        scratch_shapes=[
            pltpu.VMEM((128, 256), BF16),
            pltpu.VMEM((128, 256), BF16),
            pltpu.VMEM((8, 8, 8, 128), F32),
            pltpu.VMEM((4, 8, 8, 8, 512), F32),
            pltpu.VMEM((3, 8, 8, 8, 512), F32),
            pltpu.VMEM((8, 8, 8, 512), F32),
            pltpu.VMEM((4, 8, 8, 8, 512), F32),
            pltpu.VMEM((3, 2, 512, 512), BF16),
            pltpu.VMEM((3, 2, 2, 512, 128), BF16),
            pltpu.VMEM((3, 2, 2, 128, 512), BF16),
            pltpu.VMEM((2, 3, 2, 64, 128), F32),
            pltpu.VMEM((2, 3, 2, 64, 128), F32),
            pltpu.VMEM((bits + 1, 8, 128), F32),
            pltpu.VMEM((bits, 8, 128), F32),
            pltpu.VMEM((8, 128), F32),
            pltpu.SemaphoreType.DMA((11,)),
            pltpu.SemaphoreType.DMA((4,)),
            pltpu.SemaphoreType.DMA((2, 3, 2)),
            pltpu.SemaphoreType.DMA((2, 3, 2)),
            pltpu.SemaphoreType.DMA((bits,)),
            pltpu.SemaphoreType.DMA((bits,)),
        ],
        compiler_params=pltpu.CompilerParams(
            collective_id=0, has_side_effects=True, vmem_limit_bytes=60 * 1024 * 1024
        ),
        cost_estimate=pl.CostEstimate(flops=6 * 10**9, bytes_accessed=12 * 2**20, transcendentals=0),
    )(cotangent, base_velocity, viscosity, elem_slot, forward, backward, mass)
    return hand_over(assembled), average


def solution(mesh):
    in_specs = (
        P(None, None, None, None, ("groups", "gx")),
        P(None, None, None, None, ("groups", "gx")),
        P(None, None, None, ("groups", "gx")),
        P(("groups", "gx"), None),
    )
    out_specs = (P(None, None, None, None, ("groups", "gx")), P("groups"))
    return jax.shard_map(shards, mesh=mesh, in_specs=in_specs, out_specs=out_specs, check_vma=False)
```
